1024 devices in a mesh: dp: 16 (over y, core), expert: 64 (over x, z).
Axes of the slice: x: 8, y: 8, z: 8, core: 2. Of those that a mesh axis runs over, the one named last changes fastest.
Arguments:
- tokens: bfloat16 [131072, 1024], P(('dp', 'expert')), may hold values from -6 to 6
- expert_ids: int32 [131072, 2], P(('dp', 'expert')), may hold values from 0 to 63, all different within a row
- gate_weights: float32 [131072, 2], P(('dp', 'expert')), may hold values from 0.25 to 1
- replica_plan: int32 [64], replicated, may hold values from 0 to 1, as said below
- assignment: int32 [131072, 2], P(('dp', 'expert')), may hold values 0 or 1
- w_in: bfloat16 [64, 1024, 384], P('expert'), may hold values from -0.1875 to 0.1875
- w_out: bfloat16 [64, 384, 1024], P('expert'), may hold values from -0.3125 to 0.3125
- cotangent: bfloat16 [131072, 1024], P(('dp', 'expert')), may hold values from -6 to 6
Outputs:
- mixed: bfloat16 [131072, 1024], P(('dp', 'expert'))
- grad_tokens: bfloat16 [131072, 1024], P(('dp', 'expert'))
- grad_in: float32 [64, 1024, 384], P('expert', 'dp')
- grad_out: float32 [64, 384, 1024], P('expert', 'dp')
The draws below stay inside these ranges and needn't reach their ends.
Inputs may be any that keep to these rules, and one draw needn't show every extreme that they name: `expert_ids`: each row names 2 different experts; every expert is named by some row. `replica_plan`: expert 0 always has a copy.
All inputs are finite; a program needn't handle non-finite values. No bound on the sum of `assignment` on one device may be relied on, other than what follows from the above.
Results may differ from the reference program's by a relative error of at most 0.022.
Values may be sent and summed in bfloat16 or wider, within the bound.
A program may use at most 32 MiB of HBM per device.

```python
import jax
import jax.numpy as jnp
from jax import lax

D = 1024
FF = 384
TOP = 2
TOK_DEV = 128
EXPERTS = 64
TOKENS = 131072
CAP = 2
N_DP = 16
N_EXPERT = 64


def draw_replica_plan(key, part):
    key = jax.random.fold_in(key, 11)
    flags = jax.random.randint(key, (EXPERTS,), 0, 2, dtype=jnp.int32)
    first = (jnp.arange(EXPERTS, dtype=jnp.int32) == 0).astype(jnp.int32)
    return jnp.maximum(flags, first).astype(jnp.int32)


def touch_ends(array, own_key, smallest, top_value):
    longest = array.shape.index(max(array.shape))
    spots = []
    for shift in (0, 1):
        where = [jax.random.randint(jax.random.fold_in(own_key, axis), (), 0, length) for axis, length in enumerate(array.shape)]
        where[longest] = (where[longest] + shift) % array.shape[longest]
        spots.append(tuple(where))
    return array.at[spots[0]].set(smallest).at[spots[1]].set(top_value)


def block_levels(key, dims, split, smallest, top_value):
    factor_of = 1.0
    for dim, shards_of in split:
        draws = jax.random.uniform(jax.random.fold_in(jax.random.fold_in(key, 6), dim), (shards_of,), jnp.float32, smallest / len(split), top_value / len(split))
        factor_of = factor_of * jnp.repeat(jnp.exp(draws), dims[dim] // shards_of).reshape((-1,) + (1,) * (len(dims) - 1 - dim))
    return factor_of


def picks_of(stream_key, rows, count, top, lift):
    ranking = jax.random.permutation(jax.random.fold_in(stream_key, 1), count)
    pull = ranking
    for power in range(3):
        pull = pull * pull // count
    pull = pull * lift // count
    tickets = jax.random.randint(jax.random.fold_in(stream_key, 2), (rows, count), 0, 4096) + pull
    holders = jax.random.permutation(jax.random.fold_in(stream_key, 3), rows)[jnp.arange(count) % rows]
    tickets = jnp.where(jnp.arange(rows)[:, None] == holders[None, :], 1 << 14, tickets)
    merit = tickets * count + jnp.arange(count)
    return lax.top_k(merit.astype(jnp.int32), top)[1].astype(jnp.int32)


def gaussian(stream_key, shape, scale, bound, shards=(), kind=jnp.bfloat16):
    values = scale * jax.random.normal(stream_key, shape, jnp.float32)
    if shards:
        values = values * block_levels(stream_key, shape, shards, -0.22, 0.18)
    return jnp.clip(values, -bound, bound).astype(kind)


def setup_inputs(seed: int = 0) -> dict:
    seeds = jax.random.split(jax.random.key(seed), 9)
    return {
        "tokens": gaussian(seeds[0], (TOKENS, D), 1.0, 6.0, ((0, 1024),)),
        "expert_ids": picks_of(seeds[1], TOKENS, EXPERTS, TOP, 512),
        "gate_weights": jnp.clip(0.25 + 0.75 * jax.random.uniform(seeds[2], (TOKENS, TOP), jnp.float32) ** block_levels(seeds[2], (TOKENS, TOP), ((0, 1024),), -0.2, 0.2), 0.25, 1.0),
        "replica_plan": draw_replica_plan(jax.random.fold_in(seeds[8], 71), 0),
        "assignment": touch_ends((jax.random.randint(seeds[4], (TOKENS, TOP), 0, 2) < 1).astype(jnp.int32), jax.random.fold_in(seeds[4], 1), 0, 1),
        "w_in": gaussian(seeds[5], (EXPERTS, D, FF), D ** -0.5, 0.1875, ((0, 64),)),
        "w_out": gaussian(seeds[6], (EXPERTS, FF, D), FF ** -0.5, 0.3125, ((0, 64),)),
        "cotangent": gaussian(seeds[7], (TOKENS, D), 1.0, 6.0, ((0, 1024),)),
    }


def silu_slope(preact):
    sigmoid_pre = jax.nn.sigmoid(preact)
    return sigmoid_pre * (1.0 + preact * (1.0 - sigmoid_pre))


def rank_rows(instance_keys):
    instance_match = (instance_keys[:, None] == jnp.arange(2 * EXPERTS, dtype=jnp.int32)[None, :]).astype(jnp.int32)
    earlier = jnp.cumsum(instance_match, axis=0) - instance_match
    return jnp.sum(earlier * instance_match, axis=1)


def reference(tokens, expert_ids, gate_weights, replica_plan, assignment, w_in, w_out, cotangent):
    row_count = TOKENS * TOP
    expert_rows = expert_ids.reshape(-1)
    replica_flag = assignment.reshape(-1) * replica_plan[expert_rows]
    instance = expert_rows * 2 + replica_flag
    row_rank = lax.map(rank_rows, instance.reshape(N_DP * N_EXPERT, TOK_DEV * TOP)).reshape(-1)
    keep_mask = row_rank < CAP
    source = jnp.arange(row_count, dtype=jnp.int32) // (TOK_DEV * TOP)
    group = source // N_EXPERT
    sender = source % N_EXPERT
    total_slots = EXPERTS * N_DP * N_EXPERT * 2 * CAP
    position = (((expert_rows * N_DP + group) * N_EXPERT + sender) * 2 + replica_flag) * CAP + row_rank
    position = jnp.where(keep_mask, position, total_slots).astype(jnp.int32)
    row_ids = jnp.arange(row_count, dtype=jnp.int32)
    slot_rows = jnp.full((total_slots,), row_count, jnp.int32).at[position].set(row_ids, mode="drop")
    padded_tokens = jnp.concatenate((tokens, jnp.zeros((1, D), tokens.dtype)), axis=0)
    padded_cotangent = jnp.concatenate((cotangent, jnp.zeros((1, D), cotangent.dtype)), axis=0)
    gate_flat = jnp.concatenate((gate_weights.reshape(-1), jnp.zeros((1,), gate_weights.dtype)), axis=0)

    def one_expert(operands):
        slot_ids, weight_in, weight_out = operands
        inputs = padded_tokens[slot_ids // TOP]
        row_gate = gate_flat[slot_ids]
        preact = jnp.dot(inputs, weight_in, preferred_element_type=jnp.float32)
        hidden = jax.nn.silu(preact).astype(jnp.bfloat16)
        produced = jnp.dot(hidden, weight_out, preferred_element_type=jnp.float32).astype(jnp.bfloat16)
        scaled = (padded_cotangent[slot_ids // TOP].astype(jnp.float32) * row_gate[:, None]).astype(jnp.bfloat16)
        d_hidden = jnp.dot(scaled, weight_out.T, preferred_element_type=jnp.float32)
        d_preact = (d_hidden * silu_slope(preact)).astype(jnp.bfloat16)
        row_grads = jnp.dot(d_preact, weight_in.T, preferred_element_type=jnp.float32).astype(jnp.bfloat16)
        shape_rows = (N_DP, N_EXPERT, 2, CAP)
        part_in = jnp.einsum("gnicd,gnicf->gidf", inputs.reshape(shape_rows + (D,)).astype(jnp.float32),
                             d_preact.reshape(shape_rows + (FF,)).astype(jnp.float32)).astype(jnp.bfloat16)
        part_out = jnp.einsum("gnicf,gnicd->gifd", hidden.reshape(shape_rows + (FF,)).astype(jnp.float32),
                              scaled.reshape(shape_rows + (D,)).astype(jnp.float32)).astype(jnp.bfloat16)
        grad_in_one = jnp.sum(part_in.astype(jnp.float32), axis=(0, 1))
        grad_out_one = jnp.sum(part_out.astype(jnp.float32), axis=(0, 1))
        return produced, row_grads, grad_in_one, grad_out_one

    produced, row_grads, grad_in, grad_out = lax.map(one_expert, (slot_rows.reshape(EXPERTS, -1), w_in, w_out))
    produced = produced.reshape(total_slots, D)
    row_grads = row_grads.reshape(total_slots, D)
    token_position = position.reshape(TOKENS, TOP)
    mixed_total = jnp.zeros((TOKENS, D), jnp.float32)
    grad_total = jnp.zeros((TOKENS, D), jnp.float32)
    for choice_index in range(TOP):
        where_rows = token_position[:, choice_index]
        picked = jnp.take(produced, where_rows, axis=0, mode="fill", fill_value=0)
        picked_grad = jnp.take(row_grads, where_rows, axis=0, mode="fill", fill_value=0)
        mixed_total = mixed_total + picked.astype(jnp.float32) * gate_weights[:, choice_index][:, None]
        grad_total = grad_total + picked_grad.astype(jnp.float32)
    return mixed_total.astype(jnp.bfloat16), grad_total.astype(jnp.bfloat16), grad_in, grad_out
```

```python
import jax
import jax.numpy as jnp
from jax import lax
from jax.sharding import PartitionSpec as P


def product(form, left, right):
    return jnp.einsum(form, left, right, preferred_element_type=jnp.float32)


def local(tokens, expert_ids, gate_weights, replica_plan, assignment, w_in, w_out, cotangent):
    expert_count = lax.axis_size("expert")
    group_count = lax.axis_size("dp")
    tok_rows, model_width = tokens.shape
    top_count = expert_ids.shape[1]
    experts_total = replica_plan.shape[0]
    capacity = tok_rows * top_count // (2 * expert_count)
    row_count = tok_rows * top_count
    expert_rows = expert_ids.reshape(-1)
    expert_match = (
        expert_rows[:, None] == jnp.arange(experts_total, dtype=jnp.int32)[None, :]
    ).astype(jnp.int32)
    planned = jnp.sum(expert_match * replica_plan[None, :], axis=1)
    instance = expert_rows * 2 + assignment.reshape(-1) * planned
    instance_match = (
        instance[:, None] == jnp.arange(2 * expert_count, dtype=jnp.int32)[None, :]
    ).astype(jnp.int32)
    earlier = jnp.cumsum(instance_match, axis=0) - instance_match
    row_rank = jnp.sum(earlier * instance_match, axis=1)
    keep_mask = row_rank < capacity
    slot_total = 2 * expert_count * capacity
    slot_index = jnp.where(keep_mask, instance * capacity + row_rank, slot_total)
    row_gates = gate_weights.reshape(-1) * keep_mask.astype(jnp.float32)
    row_ids = jnp.arange(row_count, dtype=jnp.int32)
    slot_source = (
        jnp.full((slot_total,), row_count, jnp.int32).at[slot_index].set(row_ids, mode="drop")
    )
    slot_token = slot_source // top_count
    gate_slots = jnp.concatenate((row_gates, jnp.zeros((1,), jnp.float32)), axis=0)[slot_source]
    both = jnp.concatenate((tokens, cotangent), axis=1)
    both = jnp.concatenate((both, jnp.zeros((1, 2 * model_width), both.dtype)), axis=0)[slot_token]
    scaled = (both[:, model_width:].astype(jnp.float32) * gate_slots[:, None]).astype(jnp.bfloat16)
    sent = jnp.concatenate((both[:, :model_width], scaled), axis=1)

    def exchange(rows):
        blocks = rows.reshape(expert_count, 2 * capacity, 2 * model_width)
        return lax.all_to_all(blocks, "expert", 0, 0, tiled=True).reshape(slot_total, 2 * model_width)

    got = exchange(sent)
    received, arrived = got[:, :model_width], got[:, model_width:]
    preact = product("nd,df->nf", received, w_in[0])
    gate = jax.nn.sigmoid(preact)
    hidden = (preact * gate).astype(jnp.bfloat16)
    produced = product("nf,fd->nd", hidden, w_out[0]).astype(jnp.bfloat16)
    d_hidden = product("nd,fd->nf", arrived, w_out[0])
    d_preact = (d_hidden * gate * (1.0 + preact * (1.0 - gate))).astype(jnp.bfloat16)
    row_grads = product("nf,df->nd", d_preact, w_in[0]).astype(jnp.bfloat16)
    part_in = product("nd,nf->df", received, d_preact).astype(jnp.bfloat16)
    part_out = product("nf,nd->fd", hidden, arrived).astype(jnp.bfloat16)

    back = exchange(jnp.concatenate((produced, row_grads), axis=1))
    picked = jnp.take(back, slot_index, axis=0, mode="fill", fill_value=0).astype(jnp.float32)
    weighted = picked[:, :model_width] * row_gates[:, None]
    mixed = jnp.sum(weighted.reshape(tok_rows, top_count, model_width), axis=1).astype(jnp.bfloat16)
    grad_tokens = jnp.sum(
        picked[:, model_width:].reshape(tok_rows, top_count, model_width), axis=1
    ).astype(jnp.bfloat16)

    def total(part):
        blocks = part.reshape(group_count, part.shape[0] // group_count, part.shape[1])
        blocks = lax.all_to_all(blocks, "dp", 0, 0, tiled=True)
        return jnp.sum(blocks.astype(jnp.float32), axis=0)[None]

    return (mixed, grad_tokens, total(part_in), total(part_out))


def solution(mesh):
    in_specs = (
        P(("dp", "expert"), None),
        P(("dp", "expert"), None),
        P(("dp", "expert"), None),
        P(),
        P(("dp", "expert"), None),
        P("expert", None, None),
        P("expert", None, None),
        P(("dp", "expert"), None),
    )
    out_specs = (
        P(("dp", "expert"), None),
        P(("dp", "expert"), None),
        P("expert", "dp", None),
        P("expert", "dp", None),
    )
    return jax.shard_map(local, mesh=mesh, in_specs=in_specs, out_specs=out_specs, check_vma=False)
```

```python
import functools

import jax
import jax.numpy as jnp
from jax import lax
from jax.experimental import pallas as pl
from jax.experimental.pallas import tpu as pltpu
from jax.sharding import PartitionSpec as P

MESH = pl.DeviceIdType.MESH
BF16, F32, I32 = jnp.bfloat16, jnp.float32, jnp.int32
CAP = 2
SLOTS = 2 * CAP
CHUNKS = 4
BLOCK = SLOTS * CHUNKS
GROUPS = 4
STRIDE = 37


def mm(left, right, dims=((1,), (0,))):
    return lax.dot_general(left, right, (dims, ((), ())), preferred_element_type=F32)


def ones_where(mask):
    return jnp.where(mask, 1.0, 0.0).astype(BF16)


def iota(shape, dim):
    return lax.broadcasted_iota(I32, shape, dim)


def log2(n):
    return n.bit_length() - 1


def kernel(sides, n_dp, ids_ref, gates_ref, plan_ref, assign_ref, tok_hbm, cot_hbm, win_hbm, wout_hbm,
           mixed_ref, gtok_ref, gin_ref, gout_ref,
           tok, cot, win, wout, load_sem, rhs, pick, unpick, fold, unfold, spread,
           tok_send, cot_send, out_send, grad_send, tok_recv, cot_recv, out_recv, grad_recv,
           rows_in, rows_cot, pre, hid, dpre, acc0, acc1,
           part_in, part_out, pair_in, pair_out, half_in, half_out, ring_in, ring_out,
           send_sem, recv_sem, pair_send, pair_recv, ring_send, ring_recv):
    n_x, n_z = sides
    n_e = n_x * n_z
    n_y = n_dp // 2
    per = n_e // GROUPS
    rows = per * BLOCK
    live = per * SLOTS
    t, d = tok.shape
    wide = d // CHUNKS
    ff = win.shape[1]
    me, dp = lax.axis_index("expert"), lax.axis_index("dp")
    m_x, m_z = me // n_z, me % n_z
    m_y, core = dp // 2, dp % 2

    def peer(j, sign):
        off = (j * STRIDE) % n_e
        x = (m_x + sign * (off // n_z) + n_x) % n_x
        z = (m_z + sign * (off % n_z) + n_z) % n_z
        return x * n_z + z

    loads = [pltpu.make_async_copy(src, dst, load_sem.at[i]) for i, (src, dst) in enumerate(
        ((tok_hbm, tok), (cot_hbm, cot), (win_hbm.at[0], win), (wout_hbm.at[0], wout)))]
    for load in loads:
        load.start()

    barrier = pltpu.get_barrier_semaphore()

    @pl.loop(1, n_e)
    def _(j):
        pl.semaphore_signal(barrier, inc=1, device_id={"expert": peer(j, 1)}, device_id_type=MESH)

    @pl.loop(1, n_y)
    def _(j):
        pl.semaphore_signal(barrier, inc=1, device_id={"dp": ((m_y + j) % n_y) * 2 + core}, device_id_type=MESH)

    pl.semaphore_signal(barrier, inc=1, device_id={"dp": m_y * 2 + 1 - core}, device_id_type=MESH)

    plan = jnp.broadcast_to(plan_ref[...], (8, n_e)).astype(F32).astype(BF16)
    before = ones_where(iota((t, t), 0) < iota((t, t), 1))
    instances, flags, matches = [], [], []
    for k in range(2):
        ids = ids_ref[k:k + 1, :]
        match = ones_where(iota((n_e, t), 0) == ids)
        planned = mm(plan, match)[0:1, :].astype(I32)
        flag = assign_ref[k:k + 1, :] * planned
        flags.append(flag)
        matches.append(iota((2 * n_e, t), 0) == ids * 2 + flag)
    earlier = mm(ones_where(matches[0] | matches[1]), before)
    places = []
    for k in range(2):
        ids = ids_ref[k:k + 1, :]
        rank = jnp.sum(jnp.where(matches[k], earlier, 0.0), axis=0, keepdims=True).astype(I32)
        off_x = ((ids >> log2(n_z)) - m_x) & (n_x - 1)
        off_z = ((ids & (n_z - 1)) - m_z) & (n_z - 1)
        j = ((off_x * n_z + off_z) * pow(STRIDE, -1, n_e)) & (n_e - 1)
        places.append(jnp.where(rank < CAP, j * BLOCK + flags[k] * CAP + rank, -(1 << 20)))
    lanes = jnp.concatenate([places[k] + SLOTS * c for k in range(2) for c in range(CHUNKS)], axis=1)

    r, q = iota((rows, rows), 0), iota((rows, rows), 1)
    packed = ((r >> 2) & (per - 1)) * BLOCK + (r >> log2(live)) * SLOTS + (r & 3)
    fold[...] = ones_where(q == packed)
    packed = ((q >> 2) & (per - 1)) * BLOCK + (q >> log2(live)) * SLOTS + (q & 3)
    unfold[...] = ones_where(r == packed)

    def group(g):
        return pl.ds(pl.multiple_of(g * rows, rows), rows)

    def live_group(g):
        return pl.ds(pl.multiple_of(g * live, live), live)

    def send_group(g, stage, value, src, dst, sign):
        src[group(g), :] = value

        @pl.when(g == 0)
        def _():
            dst[0:BLOCK, :] = value[0:BLOCK, :]

        @pl.loop(0, per)
        def _(i):
            j = g * per + i

            @pl.when(j > 0)
            def _():
                span = pl.ds(pl.multiple_of(j * BLOCK, BLOCK), BLOCK)
                pltpu.make_async_remote_copy(
                    src_ref=src.at[span], dst_ref=dst.at[span], send_sem=send_sem.at[stage],
                    recv_sem=recv_sem.at[stage, g], device_id={"expert": peer(j, sign)}, device_id_type=MESH).start()

    def arrived(span, stage, g, dst):
        pltpu.make_async_remote_copy(
            src_ref=dst.at[span], dst_ref=dst.at[span], send_sem=send_sem.at[stage],
            recv_sem=recv_sem.at[stage, g], device_id={"expert": peer(1, 1)}, device_id_type=MESH).wait_recv()

    def wait_group(g, stage, dst):
        if per > 1:
            @pl.when(g == 0)
            def _():
                arrived(pl.ds(BLOCK, rows - BLOCK), stage, 0, dst)

        @pl.when(g > 0)
        def _():
            arrived(group(g), stage, g, dst)

    def wait_sent(stage, src, dst):
        span = pl.ds(BLOCK, (n_e - 1) * BLOCK)
        pltpu.make_async_remote_copy(
            src_ref=src.at[span], dst_ref=dst.at[span], send_sem=send_sem.at[stage],
            recv_sem=recv_sem.at[stage, 0], device_id={"expert": peer(1, 1)}, device_id_type=MESH).wait_send()

    loads[0].wait()
    for k in range(2):
        for c in range(CHUNKS):
            rhs[(k * CHUNKS + c) * t:(k * CHUNKS + c + 1) * t, :] = tok[:, c * wide:(c + 1) * wide]

    pl.semaphore_wait(barrier, n_e - 1 + n_y)

    @pl.loop(0, GROUPS)
    def _(g):
        chosen = ones_where(iota((rows, 2 * CHUNKS * t), 0) + g * rows == lanes)
        pick[group(g), :] = chosen
        send_group(g, 0, mm(chosen, rhs[...]).astype(BF16), tok_send, tok_recv, 1)

    stack_row = iota((t, t), 0)
    stack = jnp.where(stack_row == 0, places[0].astype(F32), 0.0)
    stack = jnp.where(stack_row == 1, places[1].astype(F32), stack)
    stack = jnp.where(stack_row == 2, gates_ref[0:1, :], stack)
    stack = jnp.where(stack_row == 3, gates_ref[1:2, :], stack)
    stack = stack.T
    gate_cols = [stack[:, 2 + k:3 + k] for k in range(2)]

    loads[1].wait()
    for k in range(2):
        scaled = (cot[...].astype(F32) * gate_cols[k]).astype(BF16)
        for c in range(CHUNKS):
            rhs[(k * CHUNKS + c) * t:(k * CHUNKS + c + 1) * t, :] = scaled[:, c * wide:(c + 1) * wide]

    @pl.loop(0, GROUPS)
    def _(g):
        send_group(g, 1, mm(pick[group(g), :], rhs[...]).astype(BF16), cot_send, cot_recv, 1)

    for k in range(2):
        place = stack[:, k:k + 1].astype(I32)
        for c in range(CHUNKS):
            unpick[k, c * t:(c + 1) * t, :] = ones_where(iota((t, n_e * BLOCK), 1) == place + SLOTS * c)

    per_ff = ff // n_dp
    f, q = iota((ff, 2 * ff), 0), iota((ff, 2 * ff), 1)
    shard = (f * (65536 // per_ff + 1)) >> 16
    base = (shard & 1) * ff + (shard >> 1) * (2 * per_ff) + (f - shard * per_ff)
    for h in range(2):
        spread[h] = ones_where(q == base + h * per_ff)

    def unpack(g, recv, out):
        mine = mm(fold[...], recv[group(g), :]).astype(BF16)
        for c in range(CHUNKS):
            out[live_group(g), c * wide:(c + 1) * wide] = mine[c * live:(c + 1) * live, :]

    def pack(value):
        value = value.astype(BF16)
        stacked = jnp.concatenate([value[:, c * wide:(c + 1) * wide] for c in range(CHUNKS)], axis=0)
        return mm(unfold[...], stacked).astype(BF16)

    loads[2].wait()
    loads[3].wait()

    @pl.loop(0, GROUPS)
    def _(g):
        wait_group(g, 0, tok_recv)
        unpack(g, tok_recv, rows_in)
        value = mm(rows_in[live_group(g), :], win[...])
        pre[live_group(g), :] = value
        hidden = (value * jax.nn.sigmoid(value)).astype(BF16)
        hid[live_group(g), :] = hidden
        send_group(g, 2, pack(mm(hidden, wout[...])), out_send, out_recv, -1)

    @pl.loop(0, GROUPS)
    def _(g):
        wait_group(g, 1, cot_recv)
        unpack(g, cot_recv, rows_cot)
        d_hidden = mm(rows_cot[live_group(g), :], wout[...], ((1,), (1,)))
        value = pre[live_group(g), :]
        gate = jax.nn.sigmoid(value)
        d_pre = (d_hidden * gate * (1.0 + value * (1.0 - gate))).astype(BF16)
        dpre[live_group(g), :] = d_pre
        send_group(g, 3, pack(mm(d_pre, win[...], ((1,), (1,)))), grad_send, grad_recv, -1)

    shard_in, shard_out = d // n_dp, 2 * per_ff
    total = mm(rows_in[...], dpre[...], ((0,), (0,))).astype(BF16)
    for s in range(n_dp):
        part_in[s % 2, s // 2 * shard_in:(s // 2 + 1) * shard_in, :] = total[s * shard_in:(s + 1) * shard_in, :]
    total = sum(mm(mm(hid[...], spread[h]).astype(BF16), rows_cot[:, h * d // 2:(h + 1) * d // 2], ((0,), (0,)))
                for h in range(2)).astype(BF16)
    for s in range(2):
        part_out[s] = total[s * ff:(s + 1) * ff, :]

    pair = [pltpu.make_async_remote_copy(
        src_ref=part.at[1 - core], dst_ref=other, send_sem=pair_send.at[i], recv_sem=pair_recv.at[i],
        device_id={"dp": m_y * 2 + 1 - core}, device_id_type=MESH)
        for i, (part, other) in enumerate(((part_in, pair_in), (part_out, pair_out)))]
    for copy in pair:
        copy.start()

    def gather_out(g):
        block = out_recv[group(g), :]
        return mm(unpick[0, :, group(g)], block), mm(unpick[1, :, group(g)], block)

    wait_group(0, 2, out_recv)
    acc0[...], acc1[...] = gather_out(0)

    for copy in pair:
        copy.wait_recv()
    half_in[...] = (part_in[core].astype(F32) + pair_in[...].astype(F32)).astype(BF16)
    half_out[...] = (part_out[core].astype(F32) + pair_out[...].astype(F32)).astype(BF16)

    def ring(step):
        there = (m_y + step) % n_y
        return [pltpu.make_async_remote_copy(
            src_ref=half.at[pl.ds(pl.multiple_of(there * size, 16), size)], dst_ref=got.at[step - 1],
            send_sem=ring_send.at[i], recv_sem=ring_recv.at[i],
            device_id={"dp": there * 2 + core}, device_id_type=MESH)
            for i, (half, got, size) in enumerate(((half_in, ring_in, shard_in), (half_out, ring_out, shard_out)))]

    @pl.loop(1, n_y)
    def _(step):
        for copy in ring(step):
            copy.start()

    @pl.loop(1, GROUPS)
    def _(g):
        wait_group(g, 2, out_recv)
        first, second = gather_out(g)
        acc0[...] += first
        acc1[...] += second

    for c in range(CHUNKS):
        span = slice(c * t, (c + 1) * t)
        mixed_ref[:, c * wide:(c + 1) * wide] = (
            acc0[span, :] * gate_cols[0] + acc1[span, :] * gate_cols[1]).astype(BF16)

    acc0[...] = jnp.zeros_like(acc0)

    @pl.loop(0, GROUPS)
    def _(g):
        wait_group(g, 3, grad_recv)
        acc0[...] += mm(unpick[0, :, group(g)] + unpick[1, :, group(g)], grad_recv[group(g), :])

    for c in range(CHUNKS):
        gtok_ref[:, c * wide:(c + 1) * wide] = acc0[c * t:(c + 1) * t, :].astype(BF16)

    def settle(i, half, got, wait):
        copy = pltpu.make_async_remote_copy(
            src_ref=got, dst_ref=got, send_sem=ring_send.at[i], recv_sem=ring_recv.at[i],
            device_id={"dp": m_y * 2 + 1 - core}, device_id_type=MESH)
        if wait:
            copy.wait_recv()
        else:
            copy.wait_send()

    def own(part, other, size):
        span = pl.ds(pl.multiple_of(m_y * size, 16), size)
        return part[core, span, :].astype(F32) + other[span, :].astype(F32)

    if n_y > 1:
        settle(0, half_in, ring_in, True)
    value = own(part_in, pair_in, shard_in)
    for step in range(n_y - 1):
        value += ring_in[step].astype(F32)
    gin_ref[...] = value
    if n_y > 1:
        settle(1, half_out, ring_out, True)
    value = own(part_out, pair_out, shard_out)
    for step in range(n_y - 1):
        value += ring_out[step].astype(F32)
    for h in range(2):
        gout_ref[:, h * d // 2:(h + 1) * d // 2] = value[h * per_ff:(h + 1) * per_ff, :]

    for stage, (src, dst) in enumerate(
            ((tok_send, tok_recv), (cot_send, cot_recv), (out_send, out_recv), (grad_send, grad_recv))):
        wait_sent(stage, src, dst)
    for copy in pair:
        copy.wait_send()
    if n_y > 1:
        settle(0, half_in, ring_in, False)
        settle(1, half_out, ring_out, False)


def local(sides, tokens, expert_ids, gate_weights, replica_plan, assignment, w_in, w_out, cotangent):
    n_e, n_dp = lax.axis_size("expert"), lax.axis_size("dp")
    t, d = tokens.shape
    ff = w_in.shape[2]
    n_y = n_dp // 2
    wide = d // CHUNKS
    total, live, rows = n_e * BLOCK, n_e * SLOTS, n_e // GROUPS * BLOCK
    vmem, hbm = pl.BlockSpec(memory_space=pltpu.VMEM), pl.BlockSpec(memory_space=pl.ANY)
    got_y = max(n_y - 1, 1)
    mixed, grad_tokens, grad_in, grad_out = pl.pallas_call(
        functools.partial(kernel, sides, n_dp),
        out_shape=(
            jax.ShapeDtypeStruct((t, d), BF16),
            jax.ShapeDtypeStruct((t, d), BF16),
            jax.ShapeDtypeStruct((d // n_dp, ff), F32),
            jax.ShapeDtypeStruct((ff // n_dp, d), F32),
        ),
        in_specs=[vmem] * 4 + [hbm] * 4,
        out_specs=[vmem] * 4,
        scratch_shapes=[
            pltpu.VMEM((t, d), BF16),
            pltpu.VMEM((t, d), BF16),
            pltpu.VMEM((d, ff), BF16),
            pltpu.VMEM((ff, d), BF16),
            pltpu.SemaphoreType.DMA((4,)),
            pltpu.VMEM((2 * CHUNKS * t, wide), BF16),
            pltpu.VMEM((total, 2 * CHUNKS * t), BF16),
            pltpu.VMEM((2, CHUNKS * t, total), BF16),
            pltpu.VMEM((rows, rows), BF16),
            pltpu.VMEM((rows, rows), BF16),
            pltpu.VMEM((2, ff, 2 * ff), BF16),
        ] + [pltpu.VMEM((total, wide), BF16)] * 8 + [
            pltpu.VMEM((live, d), BF16),
            pltpu.VMEM((live, d), BF16),
            pltpu.VMEM((live, ff), F32),
            pltpu.VMEM((live, ff), BF16),
            pltpu.VMEM((live, ff), BF16),
            pltpu.VMEM((CHUNKS * t, wide), F32),
            pltpu.VMEM((CHUNKS * t, wide), F32),
            pltpu.VMEM((2, d // 2, ff), BF16),
            pltpu.VMEM((2, ff, d // 2), BF16),
            pltpu.VMEM((d // 2, ff), BF16),
            pltpu.VMEM((ff, d // 2), BF16),
            pltpu.VMEM((d // 2, ff), BF16),
            pltpu.VMEM((ff, d // 2), BF16),
            pltpu.VMEM((got_y, d // n_dp, ff), BF16),
            pltpu.VMEM((got_y, 2 * ff // n_dp, d // 2), BF16),
            pltpu.SemaphoreType.DMA((4,)),
            pltpu.SemaphoreType.DMA((4, GROUPS)),
            pltpu.SemaphoreType.DMA((2,)),
            pltpu.SemaphoreType.DMA((2,)),
            pltpu.SemaphoreType.DMA((2,)),
            pltpu.SemaphoreType.DMA((2,)),
        ],
        compiler_params=pltpu.CompilerParams(
            collective_id=0, has_side_effects=True, vmem_limit_bytes=48 << 20),
    )(expert_ids.T, gate_weights.T, replica_plan[None], assignment.T, tokens, cotangent, w_in, w_out)
    return mixed, grad_tokens, grad_in[None], grad_out[None]


def solution(mesh):
    count = mesh.shape["expert"]
    n_x = 1 << (log2(count) // 2)
    in_specs = (
        P(("dp", "expert"), None),
        P(("dp", "expert"), None),
        P(("dp", "expert"), None),
        P(),
        P(("dp", "expert"), None),
        P("expert", None, None),
        P("expert", None, None),
        P(("dp", "expert"), None),
    )
    out_specs = (
        P(("dp", "expert"), None),
        P(("dp", "expert"), None),
        P("expert", "dp", None),
        P("expert", "dp", None),
    )
    return jax.shard_map(functools.partial(local, (n_x, count // n_x)), mesh=mesh, in_specs=in_specs,
                         out_specs=out_specs, check_vma=False)
```

```python
import functools

import jax
import jax.numpy as jnp
from jax import lax
from jax.experimental import pallas as pl
from jax.experimental.pallas import tpu as pltpu
from jax.sharding import PartitionSpec as P

MESH = pl.DeviceIdType.MESH
BF16, F32, I32 = jnp.bfloat16, jnp.float32, jnp.int32
CAP = 2
SLOTS = 2 * CAP
CHUNKS = 4
BLOCK = SLOTS * CHUNKS
GROUPS = 4
STRIDE = 37


def mm(left, right, dims=((1,), (0,))):
    return lax.dot_general(left, right, (dims, ((), ())), preferred_element_type=F32)


def ones_where(mask):
    return jnp.where(mask, 1.0, 0.0).astype(BF16)


def iota(shape, dim):
    return lax.broadcasted_iota(I32, shape, dim)


def log2(n):
    return n.bit_length() - 1


def kernel(sides, n_dp, ids_ref, gates_ref, plan_ref, assign_ref, tok_hbm, cot_hbm, win_hbm, wout_hbm,
           mixed_hbm, gtok_hbm, gin_hbm, gout_hbm,
           mixed_ref, gtok_ref, gin_ref, gout_ref, store_sem,
           tok, cot, win, wout, load_sem, rhs, pick, unpick, fold, unfold, spread,
           tok_send, cot_send, out_send, grad_send, tok_recv, cot_recv, out_recv, grad_recv,
           rows_in, rows_cot, pre, hid, dpre, acc0, acc1,
           part_in, part_out, pair_in, pair_out, half_in, half_out, ring_in, ring_out,
           send_sem, recv_sem, pair_send, pair_recv, ring_send, ring_recv):
    n_x, n_z = sides
    n_e = n_x * n_z
    n_y = n_dp // 2
    per = n_e // GROUPS
    rows = per * BLOCK
    live = per * SLOTS
    t, d = tok.shape
    wide = d // CHUNKS
    ff = win.shape[1]
    me, dp = lax.axis_index("expert"), lax.axis_index("dp")
    m_x, m_z = me // n_z, me % n_z
    m_y, core = dp // 2, dp % 2

    def peer(j, sign):
        off = (j * STRIDE) % n_e
        x = (m_x + sign * (off // n_z) + n_x) % n_x
        z = (m_z + sign * (off % n_z) + n_z) % n_z
        return x * n_z + z

    stores = [pltpu.make_async_copy(src, dst, store_sem.at[i]) for i, (src, dst) in enumerate(
        ((mixed_ref, mixed_hbm), (gtok_ref, gtok_hbm), (gin_ref, gin_hbm), (gout_ref, gout_hbm)))]
    loads = [pltpu.make_async_copy(src, dst, load_sem.at[i]) for i, (src, dst) in enumerate(
        ((tok_hbm, tok), (cot_hbm, cot), (win_hbm.at[0], win), (wout_hbm.at[0], wout)))]
    for load in loads:
        load.start()

    barrier = pltpu.get_barrier_semaphore()

    @pl.loop(1, n_e)
    def _(j):
        pl.semaphore_signal(barrier, inc=1, device_id={"expert": peer(j, 1)}, device_id_type=MESH)

    along_y = {1: (), 2: (1,)}.get(n_y, (1, n_y - 1))
    for step in along_y:
        pl.semaphore_signal(barrier, inc=1, device_id={"dp": ((m_y + step) % n_y) * 2 + core}, device_id_type=MESH)

    pl.semaphore_signal(barrier, inc=1, device_id={"dp": m_y * 2 + 1 - core}, device_id_type=MESH)

    plan = jnp.broadcast_to(plan_ref[...], (8, n_e)).astype(F32).astype(BF16)
    before = ones_where(iota((t, t), 0) < iota((t, t), 1))
    instances, flags, matches = [], [], []
    for k in range(2):
        ids = ids_ref[k:k + 1, :]
        match = ones_where(iota((n_e, t), 0) == ids)
        planned = mm(plan, match)[0:1, :].astype(I32)
        flag = assign_ref[k:k + 1, :] * planned
        flags.append(flag)
        matches.append(iota((2 * n_e, t), 0) == ids * 2 + flag)
    earlier = mm(ones_where(matches[0] | matches[1]), before)
    places = []
    for k in range(2):
        ids = ids_ref[k:k + 1, :]
        rank = jnp.sum(jnp.where(matches[k], earlier, 0.0), axis=0, keepdims=True).astype(I32)
        off_x = ((ids >> log2(n_z)) - m_x) & (n_x - 1)
        off_z = ((ids & (n_z - 1)) - m_z) & (n_z - 1)
        j = ((off_x * n_z + off_z) * pow(STRIDE, -1, n_e)) & (n_e - 1)
        places.append(jnp.where(rank < CAP, j * BLOCK + flags[k] * CAP + rank, -(1 << 20)))
    lanes = jnp.concatenate([places[k] + SLOTS * c for k in range(2) for c in range(CHUNKS)], axis=1)

    r, q = iota((rows, rows), 0), iota((rows, rows), 1)
    packed = ((r >> 2) & (per - 1)) * BLOCK + (r >> log2(live)) * SLOTS + (r & 3)
    fold[...] = ones_where(q == packed)
    packed = ((q >> 2) & (per - 1)) * BLOCK + (q >> log2(live)) * SLOTS + (q & 3)
    unfold[...] = ones_where(r == packed)

    def group(g):
        return pl.ds(pl.multiple_of(g * rows, rows), rows)

    def live_group(g):
        return pl.ds(pl.multiple_of(g * live, live), live)

    def send_group(g, stage, value, src, dst, sign):
        src[group(g), :] = value

        @pl.when(g == 0)
        def _():
            dst[0:BLOCK, :] = value[0:BLOCK, :]

        @pl.loop(0, per)
        def _(i):
            j = g * per + i

            @pl.when(j > 0)
            def _():
                span = pl.ds(pl.multiple_of(j * BLOCK, BLOCK), BLOCK)
                pltpu.make_async_remote_copy(
                    src_ref=src.at[span], dst_ref=dst.at[span], send_sem=send_sem.at[stage],
                    recv_sem=recv_sem.at[stage, g], device_id={"expert": peer(j, sign)}, device_id_type=MESH).start()

    def arrived(span, stage, g, dst):
        pltpu.make_async_remote_copy(
            src_ref=dst.at[span], dst_ref=dst.at[span], send_sem=send_sem.at[stage],
            recv_sem=recv_sem.at[stage, g], device_id={"expert": peer(1, 1)}, device_id_type=MESH).wait_recv()

    def wait_group(g, stage, dst):
        if per > 1:
            @pl.when(g == 0)
            def _():
                arrived(pl.ds(BLOCK, rows - BLOCK), stage, 0, dst)

        @pl.when(g > 0)
        def _():
            arrived(group(g), stage, g, dst)

    def wait_sent(stage, src, dst):
        span = pl.ds(BLOCK, (n_e - 1) * BLOCK)
        pltpu.make_async_remote_copy(
            src_ref=src.at[span], dst_ref=dst.at[span], send_sem=send_sem.at[stage],
            recv_sem=recv_sem.at[stage, 0], device_id={"expert": peer(1, 1)}, device_id_type=MESH).wait_send()

    loads[0].wait()
    for k in range(2):
        for c in range(CHUNKS):
            rhs[(k * CHUNKS + c) * t:(k * CHUNKS + c + 1) * t, :] = tok[:, c * wide:(c + 1) * wide]

    pl.semaphore_wait(barrier, n_e + len(along_y))

    @pl.loop(0, GROUPS)
    def _(g):
        chosen = ones_where(iota((rows, 2 * CHUNKS * t), 0) + g * rows == lanes)
        pick[group(g), :] = chosen
        send_group(g, 0, mm(chosen, rhs[...]).astype(BF16), tok_send, tok_recv, 1)

    stack_row = iota((t, t), 0)
    stack = jnp.where(stack_row == 0, places[0].astype(F32), 0.0)
    stack = jnp.where(stack_row == 1, places[1].astype(F32), stack)
    stack = jnp.where(stack_row == 2, gates_ref[0:1, :], stack)
    stack = jnp.where(stack_row == 3, gates_ref[1:2, :], stack)
    stack = stack.T
    gate_cols = [stack[:, 2 + k:3 + k] for k in range(2)]

    loads[1].wait()
    for k in range(2):
        scaled = (cot[...].astype(F32) * gate_cols[k]).astype(BF16)
        for c in range(CHUNKS):
            rhs[(k * CHUNKS + c) * t:(k * CHUNKS + c + 1) * t, :] = scaled[:, c * wide:(c + 1) * wide]

    @pl.loop(0, GROUPS)
    def _(g):
        send_group(g, 1, mm(pick[group(g), :], rhs[...]).astype(BF16), cot_send, cot_recv, 1)

    for k in range(2):
        place = stack[:, k:k + 1].astype(I32)
        for c in range(CHUNKS):
            unpick[k, c * t:(c + 1) * t, :] = ones_where(iota((t, n_e * BLOCK), 1) == place + SLOTS * c)

    per_ff = ff // n_dp
    f, q = iota((ff, 2 * ff), 0), iota((ff, 2 * ff), 1)
    shard = (f * (65536 // per_ff + 1)) >> 16
    base = (shard & 1) * ff + (shard >> 1) * (2 * per_ff) + (f - shard * per_ff)
    for h in range(2):
        spread[h] = ones_where(q == base + h * per_ff)

    def unpack(g, recv, out):
        mine = mm(fold[...], recv[group(g), :]).astype(BF16)
        for c in range(CHUNKS):
            out[live_group(g), c * wide:(c + 1) * wide] = mine[c * live:(c + 1) * live, :]

    def pack(value):
        value = value.astype(BF16)
        stacked = jnp.concatenate([value[:, c * wide:(c + 1) * wide] for c in range(CHUNKS)], axis=0)
        return mm(unfold[...], stacked).astype(BF16)

    loads[2].wait()
    loads[3].wait()

    @pl.loop(0, GROUPS)
    def _(g):
        wait_group(g, 0, tok_recv)
        unpack(g, tok_recv, rows_in)
        value = mm(rows_in[live_group(g), :], win[...])
        pre[live_group(g), :] = value
        hidden = (value * jax.nn.sigmoid(value)).astype(BF16)
        hid[live_group(g), :] = hidden
        send_group(g, 2, pack(mm(hidden, wout[...])), out_send, out_recv, -1)

    def backward(g):
        wait_group(g, 1, cot_recv)
        unpack(g, cot_recv, rows_cot)
        d_hidden = mm(rows_cot[live_group(g), :], wout[...], ((1,), (1,)))
        value = pre[live_group(g), :]
        gate = jax.nn.sigmoid(value)
        dpre[live_group(g), :] = (d_hidden * gate * (1.0 + value * (1.0 - gate))).astype(BF16)

    def send_grads(g):
        send_group(g, 3, pack(mm(dpre[live_group(g), :], win[...], ((1,), (1,)))), grad_send, grad_recv, -1)

    @pl.loop(0, GROUPS - 1)
    def _(g):
        backward(g)
        send_grads(g)

    backward(GROUPS - 1)

    shard_in, shard_out = d // n_dp, 2 * per_ff
    total = mm(rows_in[...], dpre[...], ((0,), (0,))).astype(BF16)
    for s in range(n_dp):
        part_in[s % 2, s // 2 * shard_in:(s // 2 + 1) * shard_in, :] = total[s * shard_in:(s + 1) * shard_in, :]
    total = sum(mm(mm(hid[...], spread[h]).astype(BF16), rows_cot[:, h * d // 2:(h + 1) * d // 2], ((0,), (0,)))
                for h in range(2)).astype(BF16)
    for s in range(2):
        part_out[s] = total[s * ff:(s + 1) * ff, :]

    pair = [pltpu.make_async_remote_copy(
        src_ref=part.at[1 - core], dst_ref=other, send_sem=pair_send.at[i], recv_sem=pair_recv.at[i],
        device_id={"dp": m_y * 2 + 1 - core}, device_id_type=MESH)
        for i, (part, other) in enumerate(((part_in, pair_in), (part_out, pair_out)))]
    for copy in pair:
        copy.start()

    send_grads(GROUPS - 1)

    for copy in pair:
        copy.wait_recv()
    half_in[...] = (part_in[core].astype(F32) + pair_in[...].astype(F32)).astype(BF16)
    half_out[...] = (part_out[core].astype(F32) + pair_out[...].astype(F32)).astype(BF16)

    hops = n_y // 2
    chains = ((1, 1, half_in, ring_in.at[0], shard_in), (2, -1, half_in, ring_in.at[1], shard_in),
              (2, 1, half_out, ring_out.at[0], shard_out), (1, -1, half_out, ring_out.at[1], shard_out))

    def hop(i, step):
        first, way, half, got, size = chains[i]
        there = (m_y + way * (hops + 1 - step) + n_y) % n_y
        mine = half.at[pl.ds(pl.multiple_of(there * size, 16), size)]
        if step > first:
            mine, term = got.at[step - 2], mine
            travel(i, step - 1, mine, got).wait_recv()
            mine[...] = (mine[...].astype(F32) + term[...].astype(F32)).astype(BF16)
        return travel(i, step, mine, got)

    def travel(i, step, src, got):
        return pltpu.make_async_remote_copy(
            src_ref=src, dst_ref=got.at[step - 1], send_sem=ring_send.at[i, step - 1],
            recv_sem=ring_recv.at[i, step - 1],
            device_id={"dp": ((m_y + chains[i][1] + n_y) % n_y) * 2 + core}, device_id_type=MESH)

    sent = []

    def advance(turn):
        for i in (0, 3, 1, 2):
            step = chains[i][0] + turn
            if step <= hops:
                sent.append(hop(i, step))
                sent[-1].start()

    acc0[...] = jnp.zeros_like(acc0)
    acc1[...] = jnp.zeros_like(acc1)

    def gather_out(g):
        wait_group(g, 2, out_recv)
        block = out_recv[group(g), :]
        acc0[...] += mm(unpick[0, :, group(g)], block)
        acc1[...] += mm(unpick[1, :, group(g)], block)

    turns = max(hops, 1)
    for turn in range(max(turns, GROUPS)):
        if turn < turns:
            advance(turn)
        if turn < GROUPS:
            gather_out(turn)

    for c in range(CHUNKS):
        span = slice(c * t, (c + 1) * t)
        mixed_ref[:, c * wide:(c + 1) * wide] = (
            acc0[span, :] * gate_cols[0] + acc1[span, :] * gate_cols[1]).astype(BF16)

    stores[0].start()
    acc0[...] = jnp.zeros_like(acc0)

    def gather_grads(g):
        wait_group(g, 3, grad_recv)
        acc0[...] += mm(unpick[0, :, group(g)] + unpick[1, :, group(g)], grad_recv[group(g), :])

    def complete(part, other, ends):
        size = chains[ends[0]][4]
        span = pl.ds(pl.multiple_of(m_y * size, 16), size)
        value = part[core, span, :].astype(F32) + other[span, :].astype(F32)
        for i in ends:
            if chains[i][0] <= hops:
                got = chains[i][3]
                travel(i, hops, got.at[hops - 1], got).wait_recv()
                value += got[hops - 1].astype(F32)
        return value

    gin_ref[...] = complete(part_in, pair_in, (0, 1))
    stores[2].start()
    value = complete(part_out, pair_out, (2, 3))
    for h in range(2):
        gout_ref[:, h * d // 2:(h + 1) * d // 2] = value[h * per_ff:(h + 1) * per_ff, :]
    stores[3].start()

    @pl.loop(0, GROUPS - 1)
    def _(g):
        gather_grads(g)

    gather_grads(GROUPS - 1)
    for c in range(CHUNKS):
        gtok_ref[:, c * wide:(c + 1) * wide] = acc0[c * t:(c + 1) * t, :].astype(BF16)
    stores[1].start()

    for stage, (src, dst) in enumerate(
            ((tok_send, tok_recv), (cot_send, cot_recv), (out_send, out_recv), (grad_send, grad_recv))):
        wait_sent(stage, src, dst)
    for copy in pair:
        copy.wait_send()
    for copy in sent:
        copy.wait_send()
    for store in stores:
        store.wait()


def through(*refs):
    sources, targets, held, sem = refs[:4], refs[4:8], refs[8:12], refs[12]
    ins = [pltpu.make_async_copy(sources[i], held[i], sem.at[0, i]) for i in range(4)]
    outs = [pltpu.make_async_copy(held[i], targets[i], sem.at[1, i]) for i in range(4)]
    for copy in ins:
        copy.start()
    for i in range(4):
        ins[i].wait()
        outs[i].start()
    for copy in outs:
        copy.wait()


def local(sides, tokens, expert_ids, gate_weights, replica_plan, assignment, w_in, w_out, cotangent):
    n_e, n_dp = lax.axis_size("expert"), lax.axis_size("dp")
    t, d = tokens.shape
    ff = w_in.shape[2]
    n_y = n_dp // 2
    wide = d // CHUNKS
    total, live, rows = n_e * BLOCK, n_e * SLOTS, n_e // GROUPS * BLOCK
    vmem, hbm = pl.BlockSpec(memory_space=pltpu.VMEM), pl.BlockSpec(memory_space=pl.ANY)
    hops = max(n_y // 2, 1)
    results = pl.pallas_call(
        functools.partial(kernel, sides, n_dp),
        out_shape=(
            jax.ShapeDtypeStruct((t, d), BF16),
            jax.ShapeDtypeStruct((t, d), BF16),
            jax.ShapeDtypeStruct((d // n_dp, ff), F32),
            jax.ShapeDtypeStruct((ff // n_dp, d), F32),
        ),
        in_specs=[vmem] * 4 + [hbm] * 4,
        out_specs=[hbm] * 4,
        scratch_shapes=[
            pltpu.VMEM((t, d), BF16),
            pltpu.VMEM((t, d), BF16),
            pltpu.VMEM((d // n_dp, ff), F32),
            pltpu.VMEM((ff // n_dp, d), F32),
            pltpu.SemaphoreType.DMA((4,)),
            pltpu.VMEM((t, d), BF16),
            pltpu.VMEM((t, d), BF16),
            pltpu.VMEM((d, ff), BF16),
            pltpu.VMEM((ff, d), BF16),
            pltpu.SemaphoreType.DMA((4,)),
            pltpu.VMEM((2 * CHUNKS * t, wide), BF16),
            pltpu.VMEM((total, 2 * CHUNKS * t), BF16),
            pltpu.VMEM((2, CHUNKS * t, total), BF16),
            pltpu.VMEM((rows, rows), BF16),
            pltpu.VMEM((rows, rows), BF16),
            pltpu.VMEM((2, ff, 2 * ff), BF16),
        ] + [pltpu.VMEM((total, wide), BF16)] * 8 + [
            pltpu.VMEM((live, d), BF16),
            pltpu.VMEM((live, d), BF16),
            pltpu.VMEM((live, ff), F32),
            pltpu.VMEM((live, ff), BF16),
            pltpu.VMEM((live, ff), BF16),
            pltpu.VMEM((CHUNKS * t, wide), F32),
            pltpu.VMEM((CHUNKS * t, wide), F32),
            pltpu.VMEM((2, d // 2, ff), BF16),
            pltpu.VMEM((2, ff, d // 2), BF16),
            pltpu.VMEM((d // 2, ff), BF16),
            pltpu.VMEM((ff, d // 2), BF16),
            pltpu.VMEM((d // 2, ff), BF16),
            pltpu.VMEM((ff, d // 2), BF16),
            pltpu.VMEM((2, hops, d // n_dp, ff), BF16),
            pltpu.VMEM((2, hops, 2 * ff // n_dp, d // 2), BF16),
            pltpu.SemaphoreType.DMA((4,)),
            pltpu.SemaphoreType.DMA((4, GROUPS)),
            pltpu.SemaphoreType.DMA((2,)),
            pltpu.SemaphoreType.DMA((2,)),
            pltpu.SemaphoreType.DMA((4, hops)),
            pltpu.SemaphoreType.DMA((4, hops)),
        ],
        compiler_params=pltpu.CompilerParams(
            collective_id=0, has_side_effects=True, vmem_limit_bytes=63 << 20),
    )(expert_ids.T, gate_weights.T, replica_plan[None], assignment.T, tokens, cotangent, w_in, w_out)
    results = pl.pallas_call(
        through,
        out_shape=tuple(jax.ShapeDtypeStruct(r.shape, r.dtype) for r in results),
        in_specs=[hbm] * 4,
        out_specs=[hbm] * 4,
        scratch_shapes=[pltpu.VMEM(r.shape, r.dtype) for r in results] + [pltpu.SemaphoreType.DMA((2, 4))],
        compiler_params=pltpu.CompilerParams(vmem_limit_bytes=63 << 20),
    )(*results)
    return results[0], results[1], results[2][None], results[3][None]


def solution(mesh):
    count = mesh.shape["expert"]
    n_x = 1 << (log2(count) // 2)
    in_specs = (
        P(("dp", "expert"), None),
        P(("dp", "expert"), None),
        P(("dp", "expert"), None),
        P(),
        P(("dp", "expert"), None),
        P("expert", None, None),
        P("expert", None, None),
        P(("dp", "expert"), None),
    )
    out_specs = (
        P(("dp", "expert"), None),
        P(("dp", "expert"), None),
        P("expert", "dp", None),
        P("expert", "dp", None),
    )
    return jax.shard_map(functools.partial(local, (n_x, count // n_x)), mesh=mesh, in_specs=in_specs,
                         out_specs=out_specs, check_vma=False)
```

```python
import functools

import jax
import jax.numpy as jnp
from jax import lax
from jax.experimental import pallas as pl
from jax.experimental.pallas import tpu as pltpu
from jax.sharding import PartitionSpec as P

MESH = pl.DeviceIdType.MESH
BF16, F32, I32 = jnp.bfloat16, jnp.float32, jnp.int32
CAP = 2
SLOTS = 2 * CAP
CHUNKS = 4
BLOCK = SLOTS * CHUNKS
GROUPS = 4
STRIDE = 37


def mm(left, right, dims=((1,), (0,))):
    return lax.dot_general(left, right, (dims, ((), ())), preferred_element_type=F32)


def ones_where(mask):
    return jnp.where(mask, 1.0, 0.0).astype(BF16)


def iota(shape, dim):
    return lax.broadcasted_iota(I32, shape, dim)


def log2(n):
    return n.bit_length() - 1


def kernel(sides, n_dp, ids_ref, gates_ref, plan_ref, assign_ref, tok_hbm, cot_hbm, win_hbm, wout_hbm,
           mixed_ref, gtok_ref, gin_ref, gout_ref,
           tok, cot, win, wout, load_sem, rhs, pick, unpick, fold, unfold, spread,
           tok_send, cot_send, out_send, grad_send, tok_recv, cot_recv, out_recv, grad_recv,
           rows_in, rows_cot, pre, hid, dpre, acc0, acc1,
           part_in, part_out, pair_in, pair_out, half_in, half_out, ring_in, ring_out,
           send_sem, recv_sem, pair_send, pair_recv, ring_send, ring_recv):
    n_x, n_z = sides
    n_e = n_x * n_z
    n_y = n_dp // 2
    per = n_e // GROUPS
    rows = per * BLOCK
    live = per * SLOTS
    t, d = tok.shape
    wide = d // CHUNKS
    ff = win.shape[1]
    me, dp = lax.axis_index("expert"), lax.axis_index("dp")
    m_x, m_z = me // n_z, me % n_z
    m_y, core = dp // 2, dp % 2

    def peer(g, i, sign):
        off = lax.rem(g * (per * STRIDE % n_e) + i * STRIDE % n_e, n_e)
        x = lax.rem(m_x + sign * lax.div(off, n_z) + n_x, n_x)
        z = lax.rem(m_z + sign * lax.rem(off, n_z) + n_z, n_z)
        return x * n_z + z

    loads = [pltpu.make_async_copy(src, dst, load_sem.at[i]) for i, (src, dst) in enumerate(
        ((tok_hbm, tok), (cot_hbm, cot), (win_hbm.at[0], win), (wout_hbm.at[0], wout)))]
    for load in loads:
        load.start()

    barrier = pltpu.get_barrier_semaphore()

    for x in range(n_x):
        for z in range(n_z):
            if x or z:
                there = lax.rem(m_x + x, n_x) * n_z + lax.rem(m_z + z, n_z)
                pl.semaphore_signal(barrier, inc=1, device_id={"expert": there}, device_id_type=MESH)

    along_y = {1: (), 2: (1,)}.get(n_y, (1, n_y - 1))
    for step in along_y:
        pl.semaphore_signal(barrier, inc=1, device_id={"dp": ((m_y + step) % n_y) * 2 + core}, device_id_type=MESH)

    pl.semaphore_signal(barrier, inc=1, device_id={"dp": m_y * 2 + 1 - core}, device_id_type=MESH)

    plan = jnp.broadcast_to(plan_ref[...], (8, n_e)).astype(F32).astype(BF16)
    before = ones_where(iota((t, t), 0) < iota((t, t), 1))
    instances, flags, matches = [], [], []
    for k in range(2):
        ids = ids_ref[k:k + 1, :]
        match = ones_where(iota((n_e, t), 0) == ids)
        planned = mm(plan, match)[0:1, :].astype(I32)
        flag = assign_ref[k:k + 1, :] * planned
        flags.append(flag)
        matches.append(iota((2 * n_e, t), 0) == ids * 2 + flag)
    earlier = mm(ones_where(matches[0] | matches[1]), before)
    places = []
    for k in range(2):
        ids = ids_ref[k:k + 1, :]
        rank = jnp.sum(jnp.where(matches[k], earlier, 0.0), axis=0, keepdims=True).astype(I32)
        off_x = ((ids >> log2(n_z)) - m_x) & (n_x - 1)
        off_z = ((ids & (n_z - 1)) - m_z) & (n_z - 1)
        j = ((off_x * n_z + off_z) * pow(STRIDE, -1, n_e)) & (n_e - 1)
        places.append(jnp.where(rank < CAP, j * BLOCK + flags[k] * CAP + rank, -(1 << 20)))
    lanes = jnp.concatenate([places[k] + SLOTS * c for k in range(2) for c in range(CHUNKS)], axis=1)

    r, q = iota((rows, rows), 0), iota((rows, rows), 1)
    packed = ((r >> 2) & (per - 1)) * BLOCK + (r >> log2(live)) * SLOTS + (r & 3)
    fold[...] = ones_where(q == packed)
    packed = ((q >> 2) & (per - 1)) * BLOCK + (q >> log2(live)) * SLOTS + (q & 3)
    unfold[...] = ones_where(r == packed)

    def group(g):
        return pl.ds(pl.multiple_of(g * rows, rows), rows)

    def live_group(g):
        return pl.ds(pl.multiple_of(g * live, live), live)

    def send_group(g, stage, value, src, dst, sign):
        src[group(g), :] = value

        @pl.when(g == 0)
        def _():
            dst[0:BLOCK, :] = value[0:BLOCK, :]

        def start(i):
            span = pl.ds(pl.multiple_of((g * per + i) * BLOCK, BLOCK), BLOCK)
            pltpu.make_async_remote_copy(
                src_ref=src.at[span], dst_ref=dst.at[span], send_sem=send_sem.at[stage],
                recv_sem=recv_sem.at[stage, g], device_id={"expert": peer(g, i, sign)},
                device_id_type=MESH).start()

        @pl.when(g > 0)
        def _():
            start(0)

        for i in range(1, per):
            start(i)

    def arrived(span, stage, g, dst):
        pltpu.make_async_remote_copy(
            src_ref=dst.at[span], dst_ref=dst.at[span], send_sem=send_sem.at[stage],
            recv_sem=recv_sem.at[stage, g], device_id={"expert": peer(0, 1, 1)}, device_id_type=MESH).wait_recv()

    def wait_group(g, stage, dst):
        if per > 1:
            @pl.when(g == 0)
            def _():
                arrived(pl.ds(BLOCK, rows - BLOCK), stage, 0, dst)

        @pl.when(g > 0)
        def _():
            arrived(group(g), stage, g, dst)

    def wait_sent(stage, src, dst):
        span = pl.ds(BLOCK, (n_e - 1) * BLOCK)
        pltpu.make_async_remote_copy(
            src_ref=src.at[span], dst_ref=dst.at[span], send_sem=send_sem.at[stage],
            recv_sem=recv_sem.at[stage, 0], device_id={"expert": peer(0, 1, 1)}, device_id_type=MESH).wait_send()

    loads[0].wait()
    for k in range(2):
        for c in range(CHUNKS):
            rhs[(k * CHUNKS + c) * t:(k * CHUNKS + c + 1) * t, :] = tok[:, c * wide:(c + 1) * wide]

    pl.semaphore_wait(barrier, n_e + len(along_y))

    @pl.loop(0, GROUPS)
    def _(g):
        chosen = ones_where(iota((rows, 2 * CHUNKS * t), 0) + g * rows == lanes)
        pick[group(g), :] = chosen
        send_group(g, 0, mm(chosen, rhs[...]).astype(BF16), tok_send, tok_recv, 1)

    stack_row = iota((t, t), 0)
    stack = jnp.where(stack_row == 0, places[0].astype(F32), 0.0)
    stack = jnp.where(stack_row == 1, places[1].astype(F32), stack)
    stack = jnp.where(stack_row == 2, gates_ref[0:1, :], stack)
    stack = jnp.where(stack_row == 3, gates_ref[1:2, :], stack)
    stack = stack.T
    gate_cols = [stack[:, 2 + k:3 + k] for k in range(2)]

    loads[1].wait()
    for k in range(2):
        scaled = (cot[...].astype(F32) * gate_cols[k]).astype(BF16)
        for c in range(CHUNKS):
            rhs[(k * CHUNKS + c) * t:(k * CHUNKS + c + 1) * t, :] = scaled[:, c * wide:(c + 1) * wide]

    @pl.loop(0, GROUPS)
    def _(g):
        send_group(g, 1, mm(pick[group(g), :], rhs[...]).astype(BF16), cot_send, cot_recv, 1)

    for k in range(2):
        place = stack[:, k:k + 1].astype(I32)
        for c in range(CHUNKS):
            unpick[k, c * t:(c + 1) * t, :] = ones_where(iota((t, n_e * BLOCK), 1) == place + SLOTS * c)

    per_ff = ff // n_dp
    f, q = iota((ff, 2 * ff), 0), iota((ff, 2 * ff), 1)
    shard = (f * (65536 // per_ff + 1)) >> 16
    base = (shard & 1) * ff + (shard >> 1) * (2 * per_ff) + (f - shard * per_ff)
    for h in range(2):
        spread[h] = ones_where(q == base + h * per_ff)

    def unpack(g, recv, out):
        mine = mm(fold[...], recv[group(g), :]).astype(BF16)
        for c in range(CHUNKS):
            out[live_group(g), c * wide:(c + 1) * wide] = mine[c * live:(c + 1) * live, :]

    def pack(value):
        value = value.astype(BF16)
        stacked = jnp.concatenate([value[:, c * wide:(c + 1) * wide] for c in range(CHUNKS)], axis=0)
        return mm(unfold[...], stacked).astype(BF16)

    loads[2].wait()
    loads[3].wait()

    @pl.loop(0, GROUPS)
    def _(g):
        wait_group(g, 0, tok_recv)
        unpack(g, tok_recv, rows_in)
        value = mm(rows_in[live_group(g), :], win[...])
        pre[live_group(g), :] = value
        hidden = (value * jax.nn.sigmoid(value)).astype(BF16)
        hid[live_group(g), :] = hidden
        send_group(g, 2, pack(mm(hidden, wout[...])), out_send, out_recv, -1)

    def backward(g):
        wait_group(g, 1, cot_recv)
        unpack(g, cot_recv, rows_cot)
        d_hidden = mm(rows_cot[live_group(g), :], wout[...], ((1,), (1,)))
        value = pre[live_group(g), :]
        gate = jax.nn.sigmoid(value)
        dpre[live_group(g), :] = (d_hidden * gate * (1.0 + value * (1.0 - gate))).astype(BF16)

    def send_grads(g):
        send_group(g, 3, pack(mm(dpre[live_group(g), :], win[...], ((1,), (1,)))), grad_send, grad_recv, -1)

    @pl.loop(0, GROUPS - 1)
    def _(g):
        backward(g)
        send_grads(g)

    backward(GROUPS - 1)

    shard_in, shard_out = d // n_dp, 2 * per_ff
    total = mm(rows_in[...], dpre[...], ((0,), (0,))).astype(BF16)
    for s in range(n_dp):
        part_in[s % 2, s // 2 * shard_in:(s // 2 + 1) * shard_in, :] = total[s * shard_in:(s + 1) * shard_in, :]
    total = sum(mm(mm(hid[...], spread[h]).astype(BF16), rows_cot[:, h * d // 2:(h + 1) * d // 2], ((0,), (0,)))
                for h in range(2)).astype(BF16)
    for s in range(2):
        part_out[s] = total[s * ff:(s + 1) * ff, :]

    pair = [pltpu.make_async_remote_copy(
        src_ref=part.at[1 - core], dst_ref=other, send_sem=pair_send.at[i], recv_sem=pair_recv.at[i],
        device_id={"dp": m_y * 2 + 1 - core}, device_id_type=MESH)
        for i, (part, other) in enumerate(((part_in, pair_in), (part_out, pair_out)))]
    for copy in pair:
        copy.start()

    send_grads(GROUPS - 1)

    for copy in pair:
        copy.wait_recv()
    half_in[...] = (part_in[core].astype(F32) + pair_in[...].astype(F32)).astype(BF16)
    half_out[...] = (part_out[core].astype(F32) + pair_out[...].astype(F32)).astype(BF16)

    hops = n_y // 2
    chains = ((1, 1, half_in, ring_in.at[0], shard_in), (2, -1, half_in, ring_in.at[1], shard_in),
              (2, 1, half_out, ring_out.at[0], shard_out), (1, -1, half_out, ring_out.at[1], shard_out))

    def hop(i, step):
        first, way, half, got, size = chains[i]
        there = (m_y + way * (hops + 1 - step) + n_y) % n_y
        mine = half.at[pl.ds(pl.multiple_of(there * size, 16), size)]
        if step > first:
            mine, term = got.at[step - 2], mine
            travel(i, step - 1, mine, got).wait_recv()
            mine[...] = (mine[...].astype(F32) + term[...].astype(F32)).astype(BF16)
        return travel(i, step, mine, got)

    def travel(i, step, src, got):
        return pltpu.make_async_remote_copy(
            src_ref=src, dst_ref=got.at[step - 1], send_sem=ring_send.at[i, step - 1],
            recv_sem=ring_recv.at[i, step - 1],
            device_id={"dp": ((m_y + chains[i][1] + n_y) % n_y) * 2 + core}, device_id_type=MESH)

    sent = []

    def advance(turn):
        for i in (0, 3, 1, 2):
            step = chains[i][0] + turn
            if step <= hops:
                sent.append(hop(i, step))
                sent[-1].start()

    acc0[...] = jnp.zeros_like(acc0)
    acc1[...] = jnp.zeros_like(acc1)

    def gather_out(g):
        wait_group(g, 2, out_recv)
        block = out_recv[group(g), :]
        acc0[...] += mm(unpick[0, :, group(g)], block)
        acc1[...] += mm(unpick[1, :, group(g)], block)

    turns = max(hops, 1)
    for turn in range(max(turns, GROUPS)):
        if turn < turns:
            advance(turn)
        if turn < GROUPS:
            gather_out(turn)

    for c in range(CHUNKS):
        span = slice(c * t, (c + 1) * t)
        mixed_ref[:, c * wide:(c + 1) * wide] = (
            acc0[span, :] * gate_cols[0] + acc1[span, :] * gate_cols[1]).astype(BF16)

    acc0[...] = jnp.zeros_like(acc0)

    def gather_grads(g):
        wait_group(g, 3, grad_recv)
        acc0[...] += mm(unpick[0, :, group(g)] + unpick[1, :, group(g)], grad_recv[group(g), :])

    def complete(part, other, ends):
        size = chains[ends[0]][4]
        span = pl.ds(pl.multiple_of(m_y * size, 16), size)
        value = part[core, span, :].astype(F32) + other[span, :].astype(F32)
        for i in ends:
            if chains[i][0] <= hops:
                got = chains[i][3]
                travel(i, hops, got.at[hops - 1], got).wait_recv()
                value += got[hops - 1].astype(F32)
        return value

    gin_ref[...] = complete(part_in, pair_in, (0, 1))
    value = complete(part_out, pair_out, (2, 3))
    for h in range(2):
        gout_ref[:, h * d // 2:(h + 1) * d // 2] = value[h * per_ff:(h + 1) * per_ff, :]

    @pl.loop(0, GROUPS - 1)
    def _(g):
        gather_grads(g)

    gather_grads(GROUPS - 1)
    for c in range(CHUNKS):
        gtok_ref[:, c * wide:(c + 1) * wide] = acc0[c * t:(c + 1) * t, :].astype(BF16)

    for stage, (src, dst) in enumerate(
            ((tok_send, tok_recv), (cot_send, cot_recv), (out_send, out_recv), (grad_send, grad_recv))):
        wait_sent(stage, src, dst)
    for copy in pair:
        copy.wait_send()
    for copy in sent:
        copy.wait_send()


def through(*refs):
    copies = [pltpu.make_async_copy(refs[i], refs[4 + i], refs[8].at[i]) for i in range(4)]
    for copy in copies:
        copy.start()
    for copy in copies:
        copy.wait()


def local(sides, tokens, expert_ids, gate_weights, replica_plan, assignment, w_in, w_out, cotangent):
    n_e, n_dp = lax.axis_size("expert"), lax.axis_size("dp")
    t, d = tokens.shape
    ff = w_in.shape[2]
    n_y = n_dp // 2
    wide = d // CHUNKS
    total, live, rows = n_e * BLOCK, n_e * SLOTS, n_e // GROUPS * BLOCK
    vmem, hbm = pl.BlockSpec(memory_space=pltpu.VMEM), pl.BlockSpec(memory_space=pl.ANY)
    hops = max(n_y // 2, 1)
    results = pl.pallas_call(
        functools.partial(kernel, sides, n_dp),
        out_shape=(
            pltpu.VMEM((t, d), BF16),
            pltpu.VMEM((t, d), BF16),
            pltpu.VMEM((d // n_dp, ff), F32),
            pltpu.VMEM((ff // n_dp, d), F32),
        ),
        in_specs=[vmem] * 4 + [hbm] * 4,
        scratch_shapes=[
            pltpu.VMEM((t, d), BF16),
            pltpu.VMEM((t, d), BF16),
            pltpu.VMEM((d, ff), BF16),
            pltpu.VMEM((ff, d), BF16),
            pltpu.SemaphoreType.DMA((4,)),
            pltpu.VMEM((2 * CHUNKS * t, wide), BF16),
            pltpu.VMEM((total, 2 * CHUNKS * t), BF16),
            pltpu.VMEM((2, CHUNKS * t, total), BF16),
            pltpu.VMEM((rows, rows), BF16),
            pltpu.VMEM((rows, rows), BF16),
            pltpu.VMEM((2, ff, 2 * ff), BF16),
        ] + [pltpu.VMEM((total, wide), BF16)] * 8 + [
            pltpu.VMEM((live, d), BF16),
            pltpu.VMEM((live, d), BF16),
            pltpu.VMEM((live, ff), F32),
            pltpu.VMEM((live, ff), BF16),
            pltpu.VMEM((live, ff), BF16),
            pltpu.VMEM((CHUNKS * t, wide), F32),
            pltpu.VMEM((CHUNKS * t, wide), F32),
            pltpu.VMEM((2, d // 2, ff), BF16),
            pltpu.VMEM((2, ff, d // 2), BF16),
            pltpu.VMEM((d // 2, ff), BF16),
            pltpu.VMEM((ff, d // 2), BF16),
            pltpu.VMEM((d // 2, ff), BF16),
            pltpu.VMEM((ff, d // 2), BF16),
            pltpu.VMEM((2, hops, d // n_dp, ff), BF16),
            pltpu.VMEM((2, hops, 2 * ff // n_dp, d // 2), BF16),
            pltpu.SemaphoreType.DMA((4,)),
            pltpu.SemaphoreType.DMA((4, GROUPS)),
            pltpu.SemaphoreType.DMA((2,)),
            pltpu.SemaphoreType.DMA((2,)),
            pltpu.SemaphoreType.DMA((4, hops)),
            pltpu.SemaphoreType.DMA((4, hops)),
        ],
        compiler_params=pltpu.CompilerParams(
            collective_id=0, has_side_effects=True, vmem_limit_bytes=62 << 20),
    )(expert_ids.T, gate_weights.T, replica_plan[None], assignment.T, tokens, cotangent, w_in, w_out)
    results = pl.pallas_call(
        through,
        out_shape=tuple(jax.ShapeDtypeStruct(r.shape, r.dtype) for r in results),
        in_specs=[vmem] * 4,
        out_specs=[hbm] * 4,
        scratch_shapes=[pltpu.SemaphoreType.DMA((4,))],
        compiler_params=pltpu.CompilerParams(vmem_limit_bytes=16 << 20),
    )(*results)
    return results[0], results[1], results[2][None], results[3][None]


def solution(mesh):
    count = mesh.shape["expert"]
    n_x = 1 << (log2(count) // 2)
    in_specs = (
        P(("dp", "expert"), None),
        P(("dp", "expert"), None),
        P(("dp", "expert"), None),
        P(),
        P(("dp", "expert"), None),
        P("expert", None, None),
        P("expert", None, None),
        P(("dp", "expert"), None),
    )
    out_specs = (
        P(("dp", "expert"), None),
        P(("dp", "expert"), None),
        P("expert", "dp", None),
        P("expert", "dp", None),
    )
    return jax.shard_map(functools.partial(local, (n_x, count // n_x)), mesh=mesh, in_specs=in_specs,
                         out_specs=out_specs, check_vma=False)
```

```python
import functools

import jax
import jax.numpy as jnp
from jax import lax
from jax.experimental import pallas as pl
from jax.experimental.pallas import tpu as pltpu
from jax.sharding import PartitionSpec as P

MESH = pl.DeviceIdType.MESH
BF16, F32, I32 = jnp.bfloat16, jnp.float32, jnp.int32
CAP = 2
SLOTS = 2 * CAP
CHUNKS = 4
BLOCK = SLOTS * CHUNKS
GROUPS = 4
STRIDE = 37


def mm(left, right, dims=((1,), (0,))):
    return lax.dot_general(left, right, (dims, ((), ())), preferred_element_type=F32)


def ones_where(mask):
    return jnp.where(mask, 1.0, 0.0).astype(BF16)


def iota(shape, dim):
    return lax.broadcasted_iota(I32, shape, dim)


def log2(n):
    return n.bit_length() - 1


def kernel(sides, n_dp, ids_hbm, gates_hbm, plan_hbm, assign_hbm, tok_hbm, cot_hbm, win_hbm, wout_hbm,
           mixed_ref, gtok_ref, gin_ref, gout_ref,
           ids_ref, gates_ref, plan_ref, assign_ref, tok, cot, win, wout, load_sem, rhs, pick, unpick, fold, unfold, spread,
           tok_send, cot_send, out_send, grad_send, tok_recv, cot_recv, out_recv, grad_recv,
           rows_in, rows_cot, pre, hid, dpre, acc0, acc1,
           part_in, part_out, pair_in, pair_out, half_in, half_out, ring_in, ring_out,
           send_sem, recv_sem, pair_send, pair_recv, ring_send, ring_recv):
    n_x, n_z = sides
    n_e = n_x * n_z
    n_y = n_dp // 2
    per = n_e // GROUPS
    rows = per * BLOCK
    live = per * SLOTS
    t, d = tok.shape
    wide = d // CHUNKS
    ff = win.shape[1]
    me, dp = lax.axis_index("expert"), lax.axis_index("dp")
    m_x, m_z = me // n_z, me % n_z
    m_y, core = dp // 2, dp % 2

    def peer(g, i, sign):
        off = lax.rem(g * (per * STRIDE % n_e) + i * STRIDE % n_e, n_e)
        x = lax.rem(m_x + sign * lax.div(off, n_z) + n_x, n_x)
        z = lax.rem(m_z + sign * lax.rem(off, n_z) + n_z, n_z)
        return x * n_z + z

    loads = [pltpu.make_async_copy(src, dst, load_sem.at[i]) for i, (src, dst) in enumerate(
        ((tok_hbm, tok), (cot_hbm, cot), (win_hbm.at[0], win), (wout_hbm.at[0], wout), (ids_hbm, ids_ref),
         (gates_hbm, gates_ref), (plan_hbm, plan_ref), (assign_hbm, assign_ref)))]
    for load in loads[4:] + loads[:4]:
        load.start()

    barrier = pltpu.get_barrier_semaphore()

    for x in range(n_x):
        for z in range(n_z):
            if x or z:
                there = lax.rem(m_x + x, n_x) * n_z + lax.rem(m_z + z, n_z)
                pl.semaphore_signal(barrier, inc=1, device_id={"expert": there}, device_id_type=MESH)

    along_y = {1: (), 2: (1,)}.get(n_y, (1, n_y - 1))
    for step in along_y:
        pl.semaphore_signal(barrier, inc=1, device_id={"dp": ((m_y + step) % n_y) * 2 + core}, device_id_type=MESH)

    pl.semaphore_signal(barrier, inc=1, device_id={"dp": m_y * 2 + 1 - core}, device_id_type=MESH)

    for load in loads[4:]:
        load.wait()
    plan = jnp.broadcast_to(plan_ref[...], (8, n_e)).astype(F32).astype(BF16)
    before = ones_where(iota((t, t), 0) < iota((t, t), 1))
    instances, flags, matches = [], [], []
    for k in range(2):
        ids = ids_ref[k:k + 1, :]
        match = ones_where(iota((n_e, t), 0) == ids)
        planned = mm(plan, match)[0:1, :].astype(I32)
        flag = assign_ref[k:k + 1, :] * planned
        flags.append(flag)
        matches.append(iota((2 * n_e, t), 0) == ids * 2 + flag)
    earlier = mm(ones_where(matches[0] | matches[1]), before)
    places = []
    for k in range(2):
        ids = ids_ref[k:k + 1, :]
        rank = jnp.sum(jnp.where(matches[k], earlier, 0.0), axis=0, keepdims=True).astype(I32)
        off_x = ((ids >> log2(n_z)) - m_x) & (n_x - 1)
        off_z = ((ids & (n_z - 1)) - m_z) & (n_z - 1)
        j = ((off_x * n_z + off_z) * pow(STRIDE, -1, n_e)) & (n_e - 1)
        places.append(jnp.where(rank < CAP, j * BLOCK + flags[k] * CAP + rank, -(1 << 20)))
    lanes = jnp.concatenate([places[k] + SLOTS * c for k in range(2) for c in range(CHUNKS)], axis=1)

    r, q = iota((rows, rows), 0), iota((rows, rows), 1)
    packed = ((r >> 2) & (per - 1)) * BLOCK + (r >> log2(live)) * SLOTS + (r & 3)
    fold[...] = ones_where(q == packed)
    packed = ((q >> 2) & (per - 1)) * BLOCK + (q >> log2(live)) * SLOTS + (q & 3)
    unfold[...] = ones_where(r == packed)

    def group(g):
        return pl.ds(pl.multiple_of(g * rows, rows), rows)

    def live_group(g):
        return pl.ds(pl.multiple_of(g * live, live), live)

    def send_group(g, stage, value, src, dst, sign):
        src[group(g), :] = value

        @pl.when(g == 0)
        def _():
            dst[0:BLOCK, :] = value[0:BLOCK, :]

        def start(i):
            span = pl.ds(pl.multiple_of((g * per + i) * BLOCK, BLOCK), BLOCK)
            pltpu.make_async_remote_copy(
                src_ref=src.at[span], dst_ref=dst.at[span], send_sem=send_sem.at[stage],
                recv_sem=recv_sem.at[stage, g], device_id={"expert": peer(g, i, sign)},
                device_id_type=MESH).start()

        @pl.when(g > 0)
        def _():
            start(0)

        for i in range(1, per):
            start(i)

    def arrived(span, stage, g, dst):
        pltpu.make_async_remote_copy(
            src_ref=dst.at[span], dst_ref=dst.at[span], send_sem=send_sem.at[stage],
            recv_sem=recv_sem.at[stage, g], device_id={"expert": peer(0, 1, 1)}, device_id_type=MESH).wait_recv()

    def wait_group(g, stage, dst):
        if per > 1:
            @pl.when(g == 0)
            def _():
                arrived(pl.ds(BLOCK, rows - BLOCK), stage, 0, dst)

        @pl.when(g > 0)
        def _():
            arrived(group(g), stage, g, dst)

    def wait_sent(stage, src, dst):
        span = pl.ds(BLOCK, (n_e - 1) * BLOCK)
        pltpu.make_async_remote_copy(
            src_ref=src.at[span], dst_ref=dst.at[span], send_sem=send_sem.at[stage],
            recv_sem=recv_sem.at[stage, 0], device_id={"expert": peer(0, 1, 1)}, device_id_type=MESH).wait_send()

    loads[0].wait()
    for k in range(2):
        for c in range(CHUNKS):
            rhs[(k * CHUNKS + c) * t:(k * CHUNKS + c + 1) * t, :] = tok[:, c * wide:(c + 1) * wide]

    pl.semaphore_wait(barrier, n_e + len(along_y))

    @pl.loop(0, GROUPS)
    def _(g):
        chosen = ones_where(iota((rows, 2 * CHUNKS * t), 0) + g * rows == lanes)
        pick[group(g), :] = chosen
        send_group(g, 0, mm(chosen, rhs[...]).astype(BF16), tok_send, tok_recv, 1)

    stack_row = iota((t, t), 0)
    stack = jnp.where(stack_row == 0, places[0].astype(F32), 0.0)
    stack = jnp.where(stack_row == 1, places[1].astype(F32), stack)
    stack = jnp.where(stack_row == 2, gates_ref[0:1, :], stack)
    stack = jnp.where(stack_row == 3, gates_ref[1:2, :], stack)
    stack = stack.T
    gate_cols = [stack[:, 2 + k:3 + k] for k in range(2)]

    loads[1].wait()
    for k in range(2):
        scaled = (cot[...].astype(F32) * gate_cols[k]).astype(BF16)
        for c in range(CHUNKS):
            rhs[(k * CHUNKS + c) * t:(k * CHUNKS + c + 1) * t, :] = scaled[:, c * wide:(c + 1) * wide]

    @pl.loop(0, GROUPS)
    def _(g):
        send_group(g, 1, mm(pick[group(g), :], rhs[...]).astype(BF16), cot_send, cot_recv, 1)

    for k in range(2):
        place = stack[:, k:k + 1].astype(I32)
        for c in range(CHUNKS):
            unpick[k, c * t:(c + 1) * t, :] = ones_where(iota((t, n_e * BLOCK), 1) == place + SLOTS * c)

    per_ff = ff // n_dp
    f, q = iota((ff, 2 * ff), 0), iota((ff, 2 * ff), 1)
    shard = (f * (65536 // per_ff + 1)) >> 16
    base = (shard & 1) * ff + (shard >> 1) * (2 * per_ff) + (f - shard * per_ff)
    for h in range(2):
        spread[h] = ones_where(q == base + h * per_ff)

    def unpack(g, recv, out):
        mine = mm(fold[...], recv[group(g), :]).astype(BF16)
        for c in range(CHUNKS):
            out[live_group(g), c * wide:(c + 1) * wide] = mine[c * live:(c + 1) * live, :]

    def pack(value):
        value = value.astype(BF16)
        stacked = jnp.concatenate([value[:, c * wide:(c + 1) * wide] for c in range(CHUNKS)], axis=0)
        return mm(unfold[...], stacked).astype(BF16)

    loads[2].wait()
    loads[3].wait()

    @pl.loop(0, GROUPS)
    def _(g):
        wait_group(g, 0, tok_recv)
        unpack(g, tok_recv, rows_in)
        value = mm(rows_in[live_group(g), :], win[...])
        pre[live_group(g), :] = value
        hidden = (value * jax.nn.sigmoid(value)).astype(BF16)
        hid[live_group(g), :] = hidden
        send_group(g, 2, pack(mm(hidden, wout[...])), out_send, out_recv, -1)

    def backward(g):
        wait_group(g, 1, cot_recv)
        unpack(g, cot_recv, rows_cot)
        d_hidden = mm(rows_cot[live_group(g), :], wout[...], ((1,), (1,)))
        value = pre[live_group(g), :]
        gate = jax.nn.sigmoid(value)
        dpre[live_group(g), :] = (d_hidden * gate * (1.0 + value * (1.0 - gate))).astype(BF16)

    def send_grads(g):
        send_group(g, 3, pack(mm(dpre[live_group(g), :], win[...], ((1,), (1,)))), grad_send, grad_recv, -1)

    @pl.loop(0, GROUPS - 1)
    def _(g):
        backward(g)
        send_grads(g)

    backward(GROUPS - 1)

    shard_in, shard_out = d // n_dp, 2 * per_ff
    total = mm(rows_in[...], dpre[...], ((0,), (0,))).astype(BF16)
    for s in range(n_dp):
        part_in[s % 2, s // 2 * shard_in:(s // 2 + 1) * shard_in, :] = total[s * shard_in:(s + 1) * shard_in, :]
    total = sum(mm(mm(hid[...], spread[h]).astype(BF16), rows_cot[:, h * d // 2:(h + 1) * d // 2], ((0,), (0,)))
                for h in range(2)).astype(BF16)
    for s in range(2):
        part_out[s] = total[s * ff:(s + 1) * ff, :]

    pair = [pltpu.make_async_remote_copy(
        src_ref=part.at[1 - core], dst_ref=other, send_sem=pair_send.at[i], recv_sem=pair_recv.at[i],
        device_id={"dp": m_y * 2 + 1 - core}, device_id_type=MESH)
        for i, (part, other) in enumerate(((part_in, pair_in), (part_out, pair_out)))]
    for copy in pair:
        copy.start()

    send_grads(GROUPS - 1)

    for copy in pair:
        copy.wait_recv()
    half_in[...] = (part_in[core].astype(F32) + pair_in[...].astype(F32)).astype(BF16)
    half_out[...] = (part_out[core].astype(F32) + pair_out[...].astype(F32)).astype(BF16)

    hops = n_y // 2
    chains = ((1, 1, half_in, ring_in.at[0], shard_in), (2, -1, half_in, ring_in.at[1], shard_in),
              (2, 1, half_out, ring_out.at[0], shard_out), (1, -1, half_out, ring_out.at[1], shard_out))

    def hop(i, step):
        first, way, half, got, size = chains[i]
        there = (m_y + way * (hops + 1 - step) + n_y) % n_y
        mine = half.at[pl.ds(pl.multiple_of(there * size, 16), size)]
        if step > first:
            mine, term = got.at[step - 2], mine
            travel(i, step - 1, mine, got).wait_recv()
            mine[...] = (mine[...].astype(F32) + term[...].astype(F32)).astype(BF16)
        return travel(i, step, mine, got)

    def travel(i, step, src, got):
        return pltpu.make_async_remote_copy(
            src_ref=src, dst_ref=got.at[step - 1], send_sem=ring_send.at[i, step - 1],
            recv_sem=ring_recv.at[i, step - 1],
            device_id={"dp": ((m_y + chains[i][1] + n_y) % n_y) * 2 + core}, device_id_type=MESH)

    sent = []

    def advance(turn):
        for i in (0, 3, 1, 2):
            step = chains[i][0] + turn
            if step <= hops:
                sent.append(hop(i, step))
                sent[-1].start()

    acc0[...] = jnp.zeros_like(acc0)
    acc1[...] = jnp.zeros_like(acc1)

    def gather_out(g):
        wait_group(g, 2, out_recv)
        block = out_recv[group(g), :]
        acc0[...] += mm(unpick[0, :, group(g)], block)
        acc1[...] += mm(unpick[1, :, group(g)], block)

    turns = max(hops, 1)
    for turn in range(max(turns, GROUPS)):
        if turn < turns:
            advance(turn)
        if turn < GROUPS:
            gather_out(turn)

    for c in range(CHUNKS):
        span = slice(c * t, (c + 1) * t)
        mixed_ref[:, c * wide:(c + 1) * wide] = (
            acc0[span, :] * gate_cols[0] + acc1[span, :] * gate_cols[1]).astype(BF16)

    acc0[...] = jnp.zeros_like(acc0)

    def gather_grads(g):
        wait_group(g, 3, grad_recv)
        acc0[...] += mm(unpick[0, :, group(g)] + unpick[1, :, group(g)], grad_recv[group(g), :])

    def complete(part, other, ends):
        size = chains[ends[0]][4]
        span = pl.ds(pl.multiple_of(m_y * size, 16), size)
        value = part[core, span, :].astype(F32) + other[span, :].astype(F32)
        for i in ends:
            if chains[i][0] <= hops:
                got = chains[i][3]
                travel(i, hops, got.at[hops - 1], got).wait_recv()
                value += got[hops - 1].astype(F32)
        return value

    gin_ref[...] = complete(part_in, pair_in, (0, 1))
    value = complete(part_out, pair_out, (2, 3))
    for h in range(2):
        gout_ref[:, h * d // 2:(h + 1) * d // 2] = value[h * per_ff:(h + 1) * per_ff, :]

    @pl.loop(0, GROUPS - 1)
    def _(g):
        gather_grads(g)

    gather_grads(GROUPS - 1)
    for c in range(CHUNKS):
        gtok_ref[:, c * wide:(c + 1) * wide] = acc0[c * t:(c + 1) * t, :].astype(BF16)

    for stage, (src, dst) in enumerate(
            ((tok_send, tok_recv), (cot_send, cot_recv), (out_send, out_recv), (grad_send, grad_recv))):
        wait_sent(stage, src, dst)
    for copy in pair:
        copy.wait_send()
    for copy in sent:
        copy.wait_send()


def through(*refs):
    copies = [pltpu.make_async_copy(refs[i], refs[4 + i], refs[8].at[i]) for i in range(4)]
    for copy in copies:
        copy.start()
    for copy in copies:
        copy.wait()


def local(sides, tokens, expert_ids, gate_weights, replica_plan, assignment, w_in, w_out, cotangent):
    n_e, n_dp = lax.axis_size("expert"), lax.axis_size("dp")
    t, d = tokens.shape
    ff = w_in.shape[2]
    n_y = n_dp // 2
    wide = d // CHUNKS
    total, live, rows = n_e * BLOCK, n_e * SLOTS, n_e // GROUPS * BLOCK
    vmem, hbm = pl.BlockSpec(memory_space=pltpu.VMEM), pl.BlockSpec(memory_space=pl.ANY)
    hops = max(n_y // 2, 1)
    results = pl.pallas_call(
        functools.partial(kernel, sides, n_dp),
        out_shape=(
            pltpu.VMEM((t, d), BF16),
            pltpu.VMEM((t, d), BF16),
            pltpu.VMEM((d // n_dp, ff), F32),
            pltpu.VMEM((ff // n_dp, d), F32),
        ),
        in_specs=[hbm] * 8,
        scratch_shapes=[
            pltpu.VMEM((2, t), I32),
            pltpu.VMEM((2, t), F32),
            pltpu.VMEM((1, n_e), I32),
            pltpu.VMEM((2, t), I32),
            pltpu.VMEM((t, d), BF16),
            pltpu.VMEM((t, d), BF16),
            pltpu.VMEM((d, ff), BF16),
            pltpu.VMEM((ff, d), BF16),
            pltpu.SemaphoreType.DMA((8,)),
            pltpu.VMEM((2 * CHUNKS * t, wide), BF16),
            pltpu.VMEM((total, 2 * CHUNKS * t), BF16),
            pltpu.VMEM((2, CHUNKS * t, total), BF16),
            pltpu.VMEM((rows, rows), BF16),
            pltpu.VMEM((rows, rows), BF16),
            pltpu.VMEM((2, ff, 2 * ff), BF16),
        ] + [pltpu.VMEM((total, wide), BF16)] * 8 + [
            pltpu.VMEM((live, d), BF16),
            pltpu.VMEM((live, d), BF16),
            pltpu.VMEM((live, ff), F32),
            pltpu.VMEM((live, ff), BF16),
            pltpu.VMEM((live, ff), BF16),
            pltpu.VMEM((CHUNKS * t, wide), F32),
            pltpu.VMEM((CHUNKS * t, wide), F32),
            pltpu.VMEM((2, d // 2, ff), BF16),
            pltpu.VMEM((2, ff, d // 2), BF16),
            pltpu.VMEM((d // 2, ff), BF16),
            pltpu.VMEM((ff, d // 2), BF16),
            pltpu.VMEM((d // 2, ff), BF16),
            pltpu.VMEM((ff, d // 2), BF16),
            pltpu.VMEM((2, hops, d // n_dp, ff), BF16),
            pltpu.VMEM((2, hops, 2 * ff // n_dp, d // 2), BF16),
            pltpu.SemaphoreType.DMA((4,)),
            pltpu.SemaphoreType.DMA((4, GROUPS)),
            pltpu.SemaphoreType.DMA((2,)),
            pltpu.SemaphoreType.DMA((2,)),
            pltpu.SemaphoreType.DMA((4, hops)),
            pltpu.SemaphoreType.DMA((4, hops)),
        ],
        compiler_params=pltpu.CompilerParams(
            collective_id=0, has_side_effects=True, vmem_limit_bytes=62 << 20),
    )(expert_ids.T, gate_weights.T, replica_plan[None], assignment.T, tokens, cotangent, w_in, w_out)
    results = pl.pallas_call(
        through,
        out_shape=tuple(jax.ShapeDtypeStruct(r.shape, r.dtype) for r in results),
        in_specs=[vmem] * 4,
        out_specs=[hbm] * 4,
        scratch_shapes=[pltpu.SemaphoreType.DMA((4,))],
        compiler_params=pltpu.CompilerParams(vmem_limit_bytes=16 << 20),
    )(*results)
    return results[0], results[1], results[2][None], results[3][None]


def solution(mesh):
    count = mesh.shape["expert"]
    n_x = 1 << (log2(count) // 2)
    in_specs = (
        P(("dp", "expert"), None),
        P(("dp", "expert"), None),
        P(("dp", "expert"), None),
        P(),
        P(("dp", "expert"), None),
        P("expert", None, None),
        P("expert", None, None),
        P(("dp", "expert"), None),
    )
    out_specs = (
        P(("dp", "expert"), None),
        P(("dp", "expert"), None),
        P("expert", "dp", None),
        P("expert", "dp", None),
    )
    return jax.shard_map(functools.partial(local, (n_x, count // n_x)), mesh=mesh, in_specs=in_specs,
                         out_specs=out_specs, check_vma=False)
```
